32 devices in a mesh: tile: 8 (over z, x), mode: 4 (over y, core).
Axes of the slice: x: 2, y: 2, z: 4, core: 2. Of those that a mesh axis runs over, the one named last changes fastest.
Arguments:
- obj_x: float32 [2, 256, 512], P(None, 'tile', 'mode'), may hold values from -6 to 6
- dual_u: float32 [2, 256, 512], P(None, 'tile', 'mode'), may hold values from -6 to 6
- probes: float32 [4, 2, 256, 256], P('mode'), may hold values from -4 to 4
- intensity: float32 [8, 256, 256], P('tile'), may hold values from 0.1 to 4
- corners: int32 [2, 8], replicated, may hold values from 0 to 256, as said below
- owner: int32 [8], replicated, may hold values from 0 to 7, as said below
- w_in: bfloat16 [9, 48, 2], replicated, may hold values from -1.5 to 1.5
- b_in: float32 [48], replicated, may hold values from -3 to 3
- w_down: bfloat16 [4, 48, 48], replicated, may hold values from -0.4375 to 0.4375
- b_down: float32 [48], replicated, may hold values from -3 to 3
- w_mid: bfloat16 [9, 48, 48], replicated, may hold values from -0.3125 to 0.3125
- b_mid: float32 [48], replicated, may hold values from -3 to 3
- w_out: bfloat16 [9, 2, 48], replicated, may hold values from -0.3125 to 0.3125
- b_out: float32 [2], replicated, may hold values from -3 to 3
Outputs:
- obj_next: float32 [2, 256, 512], P(None, 'tile', 'mode')
- aux_next: float32 [2, 256, 512], P(None, 'tile', 'mode')
- dual_next: float32 [2, 256, 512], P(None, 'tile', 'mode')
- misfit: float32 [8], P('tile')
The draws below stay inside these ranges and needn't reach their ends.
Inputs may be any that keep to these rules, and one draw needn't show every extreme that they name: Row corners lie in 0 to 0 and column corners in 0 to 256; the upper ends are reached in every draw. Every index of tile owns between 1 and 1 positions and some owns exactly 1; of the positions of one owner at most 1 have patterns that touch one block of 32 object rows held by one index of tile, and in every draw some owner and block reach 1.
All inputs are finite; a program needn't handle non-finite values.
Results may differ from the reference program's by a relative error of at most 0.01.
Values may be sent and summed in bfloat16 or wider, within the bound.
A program may use at most 128 MiB of HBM per device.

```python
import math
import jax
import jax.numpy as jnp
from jax import lax

PATCH = 256
CHANNELS = 48
TR = 32
POS_DEV = 1
MODES = 4
OBJ_H = 256
OBJ_W = 512
NPOS = 8
OWN_MOST = 1
NB = 1
SLOTS = 8
N_TILE = 8


def scan_layout(key):
    base = jax.random.fold_in(key, 11)
    keys = jax.random.split(base, 7)
    order = jax.random.permutation(keys[0], N_TILE)
    extra = jax.random.randint(keys[1], (N_TILE // 2,), 0, POS_DEV)
    extra = extra.at[0].set(POS_DEV - 1)
    loads_pair = jnp.stack([POS_DEV + extra, POS_DEV - extra], axis=1).reshape(-1)
    loads = jnp.zeros((N_TILE,), jnp.int32).at[order].set(loads_pair.astype(jnp.int32))
    slot_ids = jnp.arange(N_TILE * OWN_MOST, dtype=jnp.int32)
    slot_dev = slot_ids // OWN_MOST
    slot_rank = slot_ids % OWN_MOST
    in_use = slot_rank < loads[slot_dev]
    scores = jax.random.permutation(keys[2], N_TILE * OWN_MOST).astype(jnp.int32)
    scores = jnp.where(in_use, scores, N_TILE * OWN_MOST + slot_ids)
    picked = jnp.argsort(scores, stable=True)[:NPOS]
    owners = slot_dev[picked]
    ranks = slot_rank[picked]
    spacing = PATCH + 2 * TR
    shift = jax.random.randint(keys[3], (N_TILE,), 0, NB)
    offset = jax.random.randint(keys[4], (N_TILE,), 0, spacing)
    jitter = jax.random.randint(keys[5], (NPOS,), 0, TR)
    band = (ranks * NB // OWN_MOST + shift[owners]) % NB
    rows = jnp.minimum(band * spacing + offset[owners] + jitter, OBJ_H - PATCH).astype(jnp.int32)
    lowest = jnp.argmax(rows)
    rows = rows.at[lowest].set(OBJ_H - PATCH)
    cols = jax.random.randint(keys[6], (NPOS,), 0, OBJ_W - PATCH + 1).astype(jnp.int32)
    cols = cols.at[0].set(OBJ_W - PATCH)
    return (jnp.stack([rows, cols]).astype(jnp.int32), owners.astype(jnp.int32))


def draw_corners(key, part):
    placed, owners = scan_layout(key)
    return placed


def draw_owner(key, part):
    placed, owners = scan_layout(key)
    return owners


def steps_of(key, dims, cuts, least, high):
    def one(axis_at, shards_of):
        steps = jax.random.uniform(jax.random.fold_in(jax.random.fold_in(key, 6), axis_at), (shards_of,), jnp.float32, least / len(cuts), high / len(cuts))
        return jnp.repeat(jnp.exp(steps), dims[axis_at] // shards_of).reshape((-1,) + (1,) * (len(dims) - axis_at - 1))

    loudness = one(*cuts[0])
    for cut in cuts[1:]:
        loudness = loudness * one(*cut)
    return loudness


def noise(key, extent, scale, most, cuts=(), kind=jnp.bfloat16):
    array = jax.random.normal(key, extent, jnp.float32) * scale
    if len(cuts) > 0:
        array = steps_of(key, extent, cuts, -0.22, 0.18) * array
    return jnp.clip(array, min=-most, max=most).astype(kind)


def setup_inputs(seed: int = 0) -> dict:
    splits = jax.random.split(jax.random.key(seed), 15)
    obj_x = noise(splits[0], (2, OBJ_H, OBJ_W), 1.0, 6.0, ((1, 8), (2, 4)), jnp.float32)
    dual_u = noise(splits[1], (2, OBJ_H, OBJ_W), 0.5, 6.0, ((1, 8), (2, 4)), jnp.float32)
    probes = noise(splits[2], (MODES, 2, PATCH, PATCH), 0.25, 4.0, ((0, 4),), jnp.float32)
    intensity = jnp.clip(jnp.exp(math.log(4.0) - 3.6888794 * jax.random.uniform(splits[3], (SLOTS, PATCH, PATCH), jnp.float32) ** steps_of(splits[3], (SLOTS, PATCH, PATCH), ((0, 8),), -0.2, 0.2)), 0.1, 4.0)
    corners = draw_corners(jax.random.fold_in(splits[14], 71), 0)
    owner = draw_owner(jax.random.fold_in(splits[14], 71), 0)
    w_in = noise(splits[6], (9, CHANNELS, 2), 18 ** -0.5, 1.5)
    b_in = noise(splits[7], (CHANNELS,), 0.5, 3.0, (), jnp.float32)
    w_down = noise(splits[8], (4, CHANNELS, CHANNELS), (4 * CHANNELS) ** -0.5, 0.4375)
    b_down = noise(splits[9], (CHANNELS,), 0.5, 3.0, (), jnp.float32)
    w_mid = noise(splits[10], (9, CHANNELS, CHANNELS), (9 * CHANNELS) ** -0.5, 0.3125)
    b_mid = noise(splits[11], (CHANNELS,), 0.5, 3.0, (), jnp.float32)
    w_out = noise(splits[12], (9, 2, CHANNELS), (9 * CHANNELS) ** -0.5, 0.3125)
    b_out = noise(splits[13], (2,), 0.5, 3.0, (), jnp.float32)
    return dict(obj_x=obj_x, dual_u=dual_u, probes=probes, intensity=intensity, corners=corners, owner=owner, w_in=w_in, b_in=b_in, w_down=w_down, b_down=b_down, w_mid=w_mid, b_mid=b_mid, w_out=w_out, b_out=b_out)


rho_weight = 2.0
floor_level = 0.25

def conv_same(act, weight):
    height = act.shape[1]
    width = act.shape[2]
    padded = jnp.pad(act.astype(jnp.float32), ((0, 0), (1, 1), (1, 1)))
    kernel = weight.astype(jnp.float32)
    total = jnp.zeros((kernel.shape[1], height, width), jnp.float32)
    for tap in range(9):
        shift_row = tap // 3
        shift_col = tap % 3
        window = padded[:, shift_row:shift_row + height, shift_col:shift_col + width]
        total = total + jnp.einsum('oc,chw->ohw', kernel[tap], window)
    return total

def through_low(values):
    lowered = values.astype(jnp.bfloat16)
    return lax.optimization_barrier(lowered).astype(jnp.float32)

def reference(obj_x, dual_u, probes, intensity, corners, owner, w_in, b_in, w_down, b_down, w_mid, b_mid, w_out, b_out):
    height_all = obj_x.shape[1]
    width_all = obj_x.shape[2]
    pos_count = owner.shape[0]
    chans = w_in.shape[1]
    indices = jnp.arange(pos_count, dtype=jnp.int32)
    earlier = (owner[:, None] == owner[None, :]) & (indices[None, :] < indices[:, None])
    slot_of = (owner * OWN_MOST + lax.optimization_barrier(jnp.sum(earlier.astype(jnp.int32), axis=1))).astype(jnp.int32)
    base = obj_x + dual_u
    base_low = base.astype(jnp.bfloat16)
    first_map = jax.nn.relu(conv_same(base_low, w_in) + b_in[:, None, None]).astype(jnp.bfloat16)
    pairs = first_map.astype(jnp.float32).reshape(chans, height_all // 2, 2, width_all // 2, 2)
    down_kernel = w_down.astype(jnp.float32).reshape(2, 2, chans, chans)
    second_map = jax.nn.relu(jnp.einsum('ijoc,chiwj->ohw', down_kernel, pairs) + b_down[:, None, None]).astype(jnp.bfloat16)
    third_map = jax.nn.relu(conv_same(second_map, w_mid) + b_mid[:, None, None]).astype(jnp.bfloat16)
    upsampled = jnp.repeat(jnp.repeat(third_map.astype(jnp.float32), 2, axis=1), 2, axis=2)
    fourth_map = (upsampled + first_map.astype(jnp.float32)).astype(jnp.bfloat16)
    aux_next = base - (conv_same(fourth_map, w_out) + b_out[:, None, None])
    obj_low = obj_x.astype(jnp.bfloat16)
    probe_re = probes[:, 0]
    probe_im = probes[:, 1]
    probe_power = lax.optimization_barrier(jnp.sum(probe_re * probe_re + probe_im * probe_im, axis=0))
    anchor = jnp.zeros((), jnp.int32)

    def one_position(index):
        row = corners[0, index]
        col = corners[1, index]
        patch = lax.dynamic_slice(obj_low, (anchor, row, col), (2, PATCH, PATCH)).astype(jnp.float32)
        wave = probe_re * patch[0] - probe_im * patch[1] + 1j * (probe_re * patch[1] + probe_im * patch[0])
        far = jnp.fft.fft2(wave, norm='ortho')
        power = lax.optimization_barrier(jnp.sum(far.real * far.real + far.imag * far.imag, axis=0))
        measured = jnp.sqrt(intensity[slot_of[index]])
        amp_error = jnp.mean((jnp.sqrt(power) - measured) ** 2)
        scale = measured / jnp.sqrt(jnp.maximum(power, floor_level))
        back = jnp.fft.ifft2(far * scale, norm='ortho')
        grad_re = lax.optimization_barrier(jnp.sum(through_low(probe_re * back.real + probe_im * back.imag), axis=0))
        grad_im = lax.optimization_barrier(jnp.sum(through_low(probe_re * back.imag - probe_im * back.real), axis=0))
        return (jnp.stack([grad_re, grad_im]), amp_error)
    grads, errors = lax.map(one_position, indices)

    def add_one(acc, index):
        row = corners[0, index]
        col = corners[1, index]
        update = jnp.concatenate([grads[index], probe_power[None]], axis=0)
        old = lax.dynamic_slice(acc, (anchor, row, col), (3, PATCH, PATCH))
        return (lax.dynamic_update_slice(acc, old + update, (anchor, row, col)), index)
    totals, unused = lax.scan(add_one, jnp.zeros((3, height_all, width_all), jnp.float32), indices)
    obj_next = (totals[:2] + rho_weight * (aux_next - dual_u)) / (totals[2] + rho_weight)
    dual_next = dual_u + obj_next - aux_next
    misfit = jnp.zeros((SLOTS,), jnp.float32).at[slot_of].set(errors)
    return (obj_next, aux_next, dual_next, misfit)
```

```python
import functools
import math

import jax
import jax.numpy as jnp
import numpy as np
from jax import lax
from jax.experimental import pallas as pl
from jax.experimental.pallas import tpu as pltpu
from jax.sharding import PartitionSpec as P

HALO = 6


rho_weight = 2.0
floor_level = 0.25


def extended_2(value, sides, width):
    for axis, dim in sides:
        count, length = (lax.axis_size(axis), value.shape[dim])
        up = [(i, (i + 1) % count) for i in range(count - 1)]
        down = [(j, i) for i, j in up]
        last = lax.slice_in_dim(value, length - width, length, axis=dim)
        first = lax.slice_in_dim(value, 0, width, axis=dim)
        before = lax.ppermute(last, axis, up)
        after = lax.ppermute(first, axis, down)
        value = jnp.concatenate([before, value, after], axis=dim)
    return value


def conv_block(act, weight):
    height = act.shape[1]
    width = act.shape[2]
    padded = jnp.pad(act, ((0, 0), (1, 1), (1, 1)))
    total = jnp.zeros((weight.shape[1], height, width), jnp.float32)
    for tap in range(9):
        shift_row = tap // 3
        shift_col = tap % 3
        window = padded[:, shift_row : shift_row + height, shift_col : shift_col + width]
        total = total + jnp.einsum(
            "oc,chw->ohw", weight[tap], window, preferred_element_type=jnp.float32
        )
    return total


def dft_tables(length, sign):
    grid = (
        jnp.arange(length, dtype=jnp.int32)[:, None]
        * jnp.arange(length, dtype=jnp.int32)[None, :]
        % length
    )
    angle = 2.0 * math.pi / length * grid.astype(jnp.float32)
    factor = 1.0 / math.sqrt(length)
    return (jnp.cos(angle) * factor, sign * jnp.sin(angle) * factor)


def left_product(table, values):
    return jnp.einsum("ab,nbc->nac", table, values, precision=lax.Precision.HIGHEST)


def right_product(values, table):
    return jnp.einsum("nab,bc->nac", values, table, precision=lax.Precision.HIGHEST)


def left_apply(table_re, table_im, real_x, imag_x):
    real_out = left_product(table_re, real_x) - left_product(table_im, imag_x)
    imag_out = left_product(table_re, imag_x) + left_product(table_im, real_x)
    return (real_out, imag_out)


def right_apply(real_x, imag_x, table_re, table_im):
    real_out = right_product(real_x, table_re) - right_product(imag_x, table_im)
    imag_out = right_product(real_x, table_im) + right_product(imag_x, table_re)
    return (real_out, imag_out)


def window_plan(
    index_list,
    pos_count,
    first_strip,
    last_strip,
    row_corner,
    rows_dev,
    strips_per,
    tile_count,
    pair_most,
):
    live = index_list < pos_count
    where_pos = jnp.minimum(index_list, pos_count - 1)
    own_first = first_strip[where_pos]
    own_last = last_strip[where_pos]
    strip_of = own_first[:, None] + jnp.arange(strips_per, dtype=jnp.int32)[None, :]
    order = jnp.arange(index_list.shape[0], dtype=jnp.int32)
    before = (order[None, None, :] < order[:, None, None]) & live[None, None, :]
    hits = (
        before
        & (own_first[None, None, :] <= strip_of[:, :, None])
        & (own_last[None, None, :] >= strip_of[:, :, None])
    )
    rank_at = jnp.sum(hits.astype(jnp.int32), axis=2)
    in_use = live[:, None] & (strip_of <= own_last[:, None])
    strip_safe = jnp.minimum(strip_of, tile_count - 1)
    rank_safe = jnp.minimum(rank_at, pair_most - 1)
    offsets = row_corner[where_pos] - own_first * rows_dev
    return (live, strip_of, rank_at, in_use, strip_safe, rank_safe, offsets)


def send_slots(touches, owner, indices, pair_most, slot_count, pos_count):
    earlier_same = (
        (owner[:, None] == owner[None, :])
        & touches[None, :]
        & (indices[None, :] < indices[:, None])
    )
    send_rank = jnp.sum(earlier_same.astype(jnp.int32), axis=1)
    send_target = jnp.where(touches, owner * pair_most + send_rank, slot_count)
    send_table = (
        jnp.full((slot_count,), pos_count, jnp.int32).at[send_target].set(indices, mode="drop")
    )
    return (jnp.minimum(send_table, pos_count - 1), send_table < pos_count)


def general_device(
    obj_x,
    dual_u,
    probes,
    intensity,
    corners,
    owner,
    w_in,
    b_in,
    w_down,
    b_down,
    w_mid,
    b_mid,
    w_out,
    b_out,
):
    tile_id = lax.axis_index("tile")
    mode_id = lax.axis_index("mode")
    tile_count = lax.axis_size("tile")
    mode_count = lax.axis_size("mode")
    rows_dev = obj_x.shape[1]
    cols_dev = obj_x.shape[2]
    width_all = cols_dev * mode_count
    height_all = rows_dev * tile_count
    patch = probes.shape[-1]
    own_most = intensity.shape[0]
    pos_count = owner.shape[0]
    chans = w_in.shape[1]
    bands = max(1, (height_all - patch - rows_dev) // (patch + 2 * rows_dev))
    pair_most = (own_most + bands - 1) // bands
    slot_count = tile_count * pair_most
    strips_per = patch // rows_dev + 1
    row_corner = corners[0]
    col_corner = corners[1]
    first_strip = row_corner // rows_dev
    last_strip = (row_corner + patch - 1) // rows_dev
    indices = jnp.arange(pos_count, dtype=jnp.int32)
    touches = (first_strip <= tile_id) & (last_strip >= tile_id)
    is_mine = owner == tile_id
    up_to = is_mine[None, :] & (indices[None, :] <= indices[:, None])
    mine_rank = jnp.sum(up_to.astype(jnp.int32), axis=1) - 1
    own_index = (
        jnp.full((own_most,), pos_count, jnp.int32)
        .at[jnp.where(is_mine, mine_rank, own_most)]
        .set(indices, mode="drop")
    )
    obj_low = obj_x.astype(jnp.bfloat16)
    strip_full = lax.all_gather(obj_low, "mode", axis=2, tiled=True)
    anchor = jnp.zeros((), jnp.int32)
    den_plane = jnp.full((), 2, jnp.int32)
    table_re, table_im = dft_tables(patch, -1.0)
    all_probes = lax.all_gather(probes, "mode", axis=0, tiled=True)
    all_re = all_probes[:, 0]
    all_im = all_probes[:, 1]
    probe_power = jnp.sum(all_re * all_re + all_im * all_im, axis=0)
    earlier = (owner[:, None] == owner[None, :]) & (indices[None, :] < indices[:, None])
    pos_rank = jnp.sum(earlier.astype(jnp.int32), axis=1)
    dealt = touches & (pos_rank % mode_count == mode_id)
    slot_pos, slot_live = send_slots(dealt, owner, indices, pair_most, slot_count, pos_count)
    local_most = (own_most + mode_count - 1) // mode_count
    local_rank = mode_id + mode_count * jnp.arange(local_most, dtype=jnp.int32)
    rank_safe_local = jnp.minimum(local_rank, own_most - 1)
    local_index = jnp.where(local_rank < own_most, own_index[rank_safe_local], pos_count)
    plan = window_plan(
        local_index,
        pos_count,
        first_strip,
        last_strip,
        row_corner,
        rows_dev,
        strips_per,
        tile_count,
        pair_most,
    )
    local_live = plan[0]
    starts = col_corner[slot_pos] + 0

    def take(start):
        return lax.dynamic_slice_in_dim(strip_full, start, patch, 2)

    cut = lax.map(take, starts)
    arrived = lax.all_to_all(
        cut.reshape(tile_count, pair_most, 2, rows_dev * patch),
        "tile",
        split_axis=0,
        concat_axis=0,
        tiled=True,
    )
    strip_safe = plan[4]
    rank_safe = plan[5]
    offsets = plan[6]
    count = offsets.shape[0]
    blocks = arrived.reshape(tile_count, pair_most, 2, rows_dev, patch)
    chosen = (strip_safe * pair_most + rank_safe).reshape(-1)
    flat_blocks = blocks.reshape(slot_count, 2, rows_dev, patch)

    def choose(slot):
        return lax.dynamic_index_in_dim(flat_blocks, slot, 0, keepdims=False)

    picked = lax.map(choose, chosen).reshape(count, strips_per, 2, rows_dev, patch)
    tall = jnp.transpose(picked, (0, 2, 1, 3, 4)).reshape(count, 2, strips_per * rows_dev, patch)

    def crop(block, offset):
        return lax.dynamic_slice_in_dim(block, offset, patch, 1)

    patches = lax.map(lambda pair: crop(*pair), (tall, offsets))
    obj_re = patches[:, 0].astype(jnp.float32)[:, None]
    obj_im = patches[:, 1].astype(jnp.float32)[:, None]
    wave_re = (all_re[None] * obj_re - all_im[None] * obj_im).reshape(
        local_most * mode_count, patch, patch
    )
    wave_im = (all_re[None] * obj_im + all_im[None] * obj_re).reshape(
        local_most * mode_count, patch, patch
    )
    far_re, far_im = left_apply(table_re, table_im, wave_re, wave_im)
    far_re, far_im = right_apply(far_re, far_im, table_re, table_im)
    far_re = far_re.reshape(local_most, mode_count, patch, patch)
    far_im = far_im.reshape(local_most, mode_count, patch, patch)
    power_all = jnp.sum(far_re * far_re + far_im * far_im, axis=1)
    measured = jnp.sqrt(intensity[rank_safe_local])
    errors = jnp.mean((jnp.sqrt(power_all) - measured) ** 2, axis=(1, 2)) * local_live.astype(
        jnp.float32
    )
    misfit_local = jnp.zeros((own_most,), jnp.float32).at[local_rank].set(errors, mode="drop")
    misfit = lax.psum(misfit_local, "mode")
    scale = (measured / jnp.sqrt(jnp.maximum(power_all, floor_level)))[:, None]
    scaled_re = (far_re * scale).reshape(local_most * mode_count, patch, patch)
    scaled_im = (far_im * scale).reshape(local_most * mode_count, patch, patch)
    back_re, back_im = left_apply(table_re, -table_im, scaled_re, scaled_im)
    back_re, back_im = right_apply(back_re, back_im, table_re, -table_im)
    back_re = back_re.reshape(local_most, mode_count, patch, patch)
    back_im = back_im.reshape(local_most, mode_count, patch, patch)
    grad_re = (
        (all_re[None] * back_re + all_im[None] * back_im).astype(jnp.bfloat16).astype(jnp.float32)
    )
    grad_im = (
        (all_re[None] * back_im - all_im[None] * back_re).astype(jnp.bfloat16).astype(jnp.float32)
    )
    grad_sum = jnp.stack([jnp.sum(grad_re, axis=1), jnp.sum(grad_im, axis=1)], axis=1)
    probe_pad = jnp.pad(probe_power, ((rows_dev, rows_dev), (0, 0)))
    strip_of = plan[1]
    rank_at = plan[2]
    in_use = plan[3]
    offsets = plan[6]
    count = offsets.shape[0]
    tall = jnp.zeros((count, 2, strips_per * rows_dev, patch), grad_sum.dtype)

    def place(block, piece, offset):
        return lax.dynamic_update_slice_in_dim(block, piece, offset, 1)

    tall = jax.vmap(place)(tall, grad_sum, offsets)
    blocks = jnp.transpose(tall.reshape(count, 2, strips_per, rows_dev, patch), (0, 2, 1, 3, 4))
    target = jnp.where(in_use, strip_of * pair_most + rank_at, slot_count).reshape(-1)
    buffer = jnp.zeros((slot_count, 2, rows_dev * patch), grad_sum.dtype)
    buffer = buffer.at[target].set(
        blocks.reshape(count * strips_per, 2, rows_dev * patch), mode="drop"
    )
    back_pieces = lax.all_to_all(
        buffer.reshape(tile_count, pair_most, 2, rows_dev * patch),
        "tile",
        split_axis=0,
        concat_axis=0,
        tiled=True,
    )
    den_gate = jnp.ones((), jnp.float32)
    flat = back_pieces.reshape(slot_count, 2, rows_dev, patch)

    def add_slot(slot_no, acc):
        where_pos = slot_pos[slot_no]
        alive = slot_live[slot_no].astype(jnp.float32)
        col = col_corner[where_pos]
        piece = flat[slot_no] * alive
        row_start = tile_id * rows_dev - row_corner[where_pos] + rows_dev
        weight_rows = lax.dynamic_slice_in_dim(probe_pad, row_start, rows_dev, 0) * (
            alive * den_gate
        )
        old_num = lax.dynamic_slice(acc, (anchor, anchor, col + 0), (2, rows_dev, patch))
        acc = lax.dynamic_update_slice(acc, old_num + piece, (anchor, anchor, col + 0))
        old_den = lax.dynamic_slice(acc, (den_plane, anchor, col), (1, rows_dev, patch))
        return lax.dynamic_update_slice(acc, old_den + weight_rows[None], (den_plane, anchor, col))

    start_acc = jnp.zeros((3, rows_dev, width_all), jnp.float32)
    acc_rows = lax.fori_loop(0, slot_count, add_slot, start_acc)
    totals = lax.psum_scatter(acc_rows, "mode", scatter_dimension=2, tiled=True)
    base = obj_x + dual_u
    extended = extended_2(base.astype(jnp.bfloat16), (("tile", 1), ("mode", 2)), HALO)
    ext_rows = rows_dev + 2 * HALO
    ext_cols = cols_dev + 2 * HALO
    row_ids = tile_id * rows_dev - HALO + jnp.arange(ext_rows, dtype=jnp.int32)
    col_ids = mode_id * cols_dev - HALO + jnp.arange(ext_cols, dtype=jnp.int32)
    row_inside = (row_ids >= 0) & (row_ids < height_all)
    col_inside = (col_ids >= 0) & (col_ids < width_all)
    fine_mask = (row_inside[:, None] & col_inside[None, :]).astype(jnp.float32)
    coarse_mask = fine_mask[::2, ::2]
    first_map = (jax.nn.relu(conv_block(extended, w_in) + b_in[:, None, None]) * fine_mask).astype(
        jnp.bfloat16
    )
    pairs = first_map.reshape(chans, ext_rows // 2, 2, ext_cols // 2, 2)
    down_kernel = w_down.reshape(2, 2, chans, chans)
    coarse = jnp.einsum("ijoc,chiwj->ohw", down_kernel, pairs, preferred_element_type=jnp.float32)
    second_map = (jax.nn.relu(coarse + b_down[:, None, None]) * coarse_mask).astype(jnp.bfloat16)
    third_map = jax.nn.relu(conv_block(second_map, w_mid) + b_mid[:, None, None]).astype(
        jnp.bfloat16
    )
    upsampled = jnp.repeat(jnp.repeat(third_map.astype(jnp.float32), 2, axis=1), 2, axis=2)
    fourth_map = (upsampled * fine_mask + first_map.astype(jnp.float32)).astype(jnp.bfloat16)
    denoised = conv_block(fourth_map, w_out) + b_out[:, None, None]
    center = denoised[:, HALO : HALO + rows_dev, HALO : HALO + cols_dev]
    aux_next = base - center
    obj_next = (totals[0:2] + rho_weight * (aux_next - dual_u)) / (totals[2] + rho_weight)
    dual_next = dual_u + obj_next - aux_next
    return (obj_next, aux_next, dual_next, misfit)


def split_bf16(values):
    high = values.astype(jnp.bfloat16)
    low = (values - high.astype(jnp.float32)).astype(jnp.bfloat16)
    return (high, low)


def dot_f32(left, right):
    return jnp.dot(left, right, preferred_element_type=jnp.float32)


def dot_split(left, right):
    return (
        dot_f32(left[0], right[0]) + dot_f32(left[0], right[1]) + dot_f32(left[1], right[0])
    )


def table_parts(length):
    grid = np.arange(length)[:, None] * np.arange(length)[None, :] % length
    angle = 2.0 * np.pi / length * grid
    cos = np.cos(angle) / math.sqrt(length)
    sin = -np.sin(angle) / math.sqrt(length)
    left = np.block([[cos, -sin], [sin, cos]]).astype(np.float32)
    right = np.block([[cos, sin], [-sin, cos]]).astype(np.float32)
    parts = []
    for table in (left, right):
        high = table.astype(jnp.bfloat16)
        low = (table - high.astype(np.float32)).astype(jnp.bfloat16)
        parts += [high, low]
    return parts


def tap_phases():
    phases = np.zeros((9, 4, 9, 4), np.float32)
    for tap in range(9):
        for i in range(2):
            for j in range(2):
                a = i + tap // 3 - 1
                b = j + tap % 3 - 1
                s = (a // 2 + 1) * 3 + b // 2 + 1
                phases[tap, 2 * i + j, s, a % 2 * 2 + b % 2] = 1.0
    return phases


MESH = pl.DeviceIdType.MESH


def fast_kernel(
    tiles,
    modes,
    corners,
    owner,
    b_out,
    obj,
    dual,
    probes,
    intensity,
    left_hi,
    left_lo,
    right_hi,
    right_lo,
    w_in,
    b_in,
    w_down,
    b_down,
    w_mid,
    b_mid,
    w_out,
    obj_next,
    aux_next,
    dual_next,
    misfit,
    gath,
    ext,
    pows,
    pow_in,
    planes,
    phase_in,
    phase_out,
    conv,
    far_s,
    p1,
    p1_in,
    p2,
    p2_in,
    back_hi,
    back_lo,
    canvas,
    c_in,
    half,
    half_in,
    mine,
    rows_in,
    a_send,
    a_recv,
    b_send,
    b_recv,
    y_send,
    y_recv,
    f_send,
    f_recv,
    h_send,
    h_recv,
    w_send,
    w_recv,
    p1_send,
    p1_recv,
    p2_send,
    p2_recv,
    g1_send,
    g1_recv,
    g2_send,
    g2_recv,
    g3_send,
    g3_recv,
):
    f32 = jnp.float32
    bf16 = jnp.bfloat16
    t = lax.axis_index("tile")
    m = lax.axis_index("mode")
    rows, cols = obj.shape[1], obj.shape[2]
    patch = intensity.shape[1]
    positions = owner.shape[0]
    core = lax.rem(m, 2)
    row = m // 2
    mate = m + 1 - 2 * core
    cross = lax.rem(m + 2, modes)
    cross_mate = lax.rem(mate + 2, modes)
    quarters = p1.shape[0]
    part = patch // quarters
    coarse_rows = rows // 2 + HALO
    lanes = coarse_rows * cols
    edge = (ext.shape[2] - rows) // 2

    def around(index, step, count):
        return lax.rem(index + step + count, count)

    barrier = pltpu.get_barrier_semaphore()
    greeted = [(around(t, d, tiles), m) for d in range(1, tiles)]
    greeted += [(t, around(m, d, modes)) for d in range(1, modes)]
    greeted += [(around(t, a, tiles), around(m, b, modes)) for a in (-1, 1) for b in (-1, 1)]
    for who in greeted:
        pl.semaphore_signal(barrier, inc=1, device_id=who, device_id_type=MESH)

    gath[m, t] = obj[...].astype(bf16)
    ext[1, :, edge : edge + rows, :] = (obj[...] + dual[...]).astype(bf16)
    row_start = pl.multiple_of(t * rows, rows)
    probe_re = probes[0, 0, pl.ds(row_start, rows), :]
    probe_im = probes[0, 1, pl.ds(row_start, rows), :]
    pows[...] = probe_re * probe_re + probe_im * probe_im

    pl.semaphore_wait(barrier, len(greeted))

    sent = []

    def remote(source, target, send, recv, who):
        return pltpu.make_async_remote_copy(
            src_ref=source,
            dst_ref=target,
            send_sem=send,
            recv_sem=recv,
            device_id=who,
            device_id_type=MESH,
        )

    def launch(*args):
        copy = remote(*args)
        copy.start()
        sent.append(copy)
        return copy

    def block_copy(source):
        return remote(gath.at[m, source], gath.at[m, source], a_send.at[0], a_recv.at[source], (t, mate))

    halo = []
    for a in (-1, 0, 1):
        for b in (-1, 0, 1):
            if a == 0 and b == 0:
                continue
            if a == 1:
                source = ext.at[1, :, rows : rows + edge, :]
                target = ext.at[1 - b, :, 0:edge, :]
            elif a == -1:
                source = ext.at[1, :, edge : 2 * edge, :]
                target = ext.at[1 - b, :, edge + rows : 2 * edge + rows, :]
            else:
                source = ext.at[1, :, edge : edge + rows, :]
                target = ext.at[1 - b, :, edge : edge + rows, :]
            who = (around(t, a, tiles), around(m, b, modes))
            number = len(halo)
            halo.append(launch(source, target, h_send.at[number], h_recv.at[number], who))
    for d in range(1, tiles):
        launch(
            gath.at[m, t], gath.at[m, t], a_send.at[d], a_recv.at[t], (around(t, d, tiles), m)
        )

    def spread(source):
        block = gath.at[m, source]
        near = launch(block, block, b_send.at[source], b_recv.at[source], (t, mate))
        over = launch(block, block, y_send.at[source], y_recv.at[source], (t, cross))
        return (near, over)

    order = [around(t, d, tiles) for d in range(tiles)]
    spreads = [spread(t)]
    weights_in = []
    for d in range(1, modes):
        weights_in.append(
            launch(
                pows, pow_in.at[d - 1], w_send.at[d - 1], w_recv.at[d - 1], (t, around(m, d, modes))
            )
        )

    for copy in halo:
        copy.wait_recv()
    line = lax.broadcasted_iota(jnp.int32, (cols, cols), 0)
    place = lax.broadcasted_iota(jnp.int32, (cols, cols), 1)
    wide = cols // 2 + HALO
    for j in range(2):
        plane = None
        for b in range(3):
            pick = (b * cols + line == cols - HALO + j + 2 * place) & (place < wide)
            block = ext[b].reshape(-1, cols)
            term = dot_f32(block, pick.astype(f32).astype(bf16))
            plane = term if plane is None else plane + term
        planes[2 * j : 2 * j + 2] = plane.reshape(2, -1, cols)
    for y in range(coarse_rows):
        first = edge - HALO + 2 * y
        phase_in[0:4, y * cols : (y + 1) * cols] = planes[:, first, :]
        phase_in[4:8, y * cols : (y + 1) * cols] = planes[:, first + 1, :]
    spot = lax.broadcasted_iota(jnp.int32, (1, lanes), 1)
    coarse_y = t * (rows // 2) - HALO // 2 + spot // cols
    coarse_x = m * (cols // 2) - HALO // 2 + spot % cols
    inside = (coarse_y >= 0) & (coarse_y < tiles * rows // 2)
    inside = inside & (coarse_x >= 0) & (coarse_x < modes * cols // 2) & (spot % cols < wide)
    mask = inside.astype(f32)

    def moved(value, s):
        offset = (s // 3 - 1) * cols + s % 3 - 1
        return value if offset == 0 else pltpu.roll(value, (-offset) % lanes, 1)

    inputs = phase_in[...] * mask
    stacked = jnp.concatenate([moved(inputs, s) for s in range(9)], axis=0).astype(bf16)
    first_map = jnp.maximum(dot_f32(w_in[...], stacked) + b_in[...], 0.0).astype(bf16)
    second_map = jnp.maximum(dot_f32(w_down[...], first_map) + b_down[...], 0.0) * mask

    for d in range(1, tiles):
        block_copy(order[d]).wait_recv()
        spreads.append(spread(order[d]))

    second_map = second_map.astype(bf16).astype(f32)
    stacked = jnp.concatenate([moved(second_map, s).astype(bf16) for s in range(9)], axis=0)
    third_map = jnp.maximum(dot_f32(w_mid[...], stacked) + b_mid[...], 0.0)
    third_map = third_map.astype(bf16).astype(f32)

    forwards = []
    for d in range(tiles):
        spreads[d][1].wait_recv()
        block = gath.at[cross, order[d]]
        forwards.append(launch(block, block, f_send.at[order[d]], f_recv.at[order[d]], (t, mate)))

    fourth_map = (
        (jnp.concatenate([third_map] * 4, axis=0) + first_map.astype(f32)) * mask
    ).astype(bf16)
    shares = dot_f32(w_out[...], fourth_map)
    total = None
    for s in range(9):
        term = moved(shares[8 * s : 8 * s + 8], s)
        total = term if total is None else total + term
    margin = HALO // 2
    for y in range(rows // 2):
        phase_out[:, y, :] = total[:, (y + margin) * cols : (y + margin + 1) * cols]
    for i in range(2):
        merged = None
        for j in range(2):
            pick = (place == 2 * (line - margin) + j).astype(f32).astype(bf16)
            value = phase_out[4 * i + 2 * j : 4 * i + 2 * j + 2].reshape(rows, cols)
            high, low = split_bf16(value)
            term = dot_f32(high, pick) + dot_f32(low, pick)
            merged = term if merged is None else merged + term
        for o in range(2):
            conv[o, pl.ds(i, rows // 2, stride=2), :] = merged[
                o * (rows // 2) : (o + 1) * (rows // 2)
            ]
    for o in range(2):
        aux_next[o] = obj[o] + dual[o] - (conv[o] + b_out[o])

    for copy in weights_in:
        copy.wait_recv()
    probe_power = pows[...]
    for d in range(1, modes):
        probe_power = probe_power + pow_in[d - 1]
    shift = (
        m * cols
        + lax.broadcasted_iota(jnp.int32, (patch, cols), 1)
        - lax.broadcasted_iota(jnp.int32, (patch, cols), 0)
    )
    times = jnp.zeros((patch, cols), f32)
    col = jnp.int32(0)
    for k in range(positions):
        times = times + (shift == corners[1, k]).astype(f32)
        col = col + jnp.where(owner[k] == t, corners[1, k], 0)
    times = times.astype(bf16)
    high, low = split_bf16(probe_power)
    denom = dot_f32(high, times) + dot_f32(low, times)

    window = (
        lax.broadcasted_iota(jnp.int32, (patch, modes * cols), 1)
        == lax.broadcasted_iota(jnp.int32, (patch, modes * cols), 0) + col
    )
    window = window.astype(f32).astype(bf16)
    for d in range(tiles):
        spreads[d][0].wait_recv()
        forwards[d].wait_recv()
    cut = []
    for plane in range(2):
        value = None
        for b in range(modes):
            block = gath[b, :, plane].reshape(patch, cols)
            term = lax.dot_general(
                block,
                window[:, b * cols : (b + 1) * cols],
                (((1,), (1,)), ((), ())),
                preferred_element_type=f32,
            )
            value = term if value is None else value + term
        cut.append(value)
    wave = jnp.concatenate(
        [
            probes[0, 0] * cut[0] - probes[0, 1] * cut[1],
            probes[0, 0] * cut[1] + probes[0, 1] * cut[0],
        ],
        axis=0,
    )
    side = dot_split((left_hi[...], left_lo[...]), split_bf16(wave))
    side = split_bf16(jnp.concatenate([side[:patch], side[patch:]], axis=1))
    right = (right_hi[...], right_lo[...])
    left = (left_hi[...], left_lo[...])
    near = []
    for q in range(quarters):
        at = slice(q * part, (q + 1) * part)
        far = dot_split((side[0][at], side[1][at]), right)
        far_s[at] = far
        p1[q] = (far[:, :patch] * far[:, :patch] + far[:, patch:] * far[:, patch:]).astype(bf16)
        near.append(launch(p1.at[q], p1_in.at[q], p1_send.at[q], p1_recv.at[q], (t, mate)))
    over = []
    for q in range(quarters):
        near[q].wait_recv()
        p2[q] = (p1[q].astype(f32) + p1_in[q].astype(f32)).astype(bf16)
        over.append(launch(p2.at[q], p2_in.at[q], p2_send.at[q], p2_recv.at[q], (t, cross)))
    errors = jnp.zeros((part, patch), f32)
    for q in range(quarters):
        at = slice(q * part, (q + 1) * part)
        over[q].wait_recv()
        power = p2[q].astype(f32) + p2_in[q].astype(f32)
        measured = jnp.sqrt(intensity[0, at])
        gap = jnp.sqrt(power) - measured
        errors = errors + gap * gap
        scale = measured * lax.rsqrt(jnp.maximum(power, floor_level))
        scaled = far_s[at] * jnp.concatenate([scale, scale], axis=1)
        back = dot_split(split_bf16(scaled), left)
        for plane in range(2):
            high, low = split_bf16(back[:, plane * patch : (plane + 1) * patch])
            to = slice(plane * patch + q * part, plane * patch + (q + 1) * part)
            back_hi[to] = high
            back_lo[to] = low
    misfit[0] = jnp.sum(errors) * (1.0 / (patch * patch))

    back = (back_hi[...], back_lo[...])
    near = []
    for q in range(quarters):
        at = slice(q * part, (q + 1) * part)
        below = slice(patch + q * part, patch + (q + 1) * part)
        value_re = dot_split((right_hi[at], right_lo[at]), back)
        value_im = dot_split((right_hi[below], right_lo[below]), back)
        re = probes[0, 0, at]
        im = probes[0, 1, at]
        grad = jnp.concatenate(
            [re * value_re + im * value_im, re * value_im - im * value_re], axis=0
        ).astype(bf16)
        spread_out = dot_f32(grad, window).astype(bf16)
        for b in range(modes):
            canvas[q, b % 2, b // 2] = spread_out[:, b * cols : (b + 1) * cols]
        near.append(
            launch(
                canvas.at[q, 1 - core], c_in.at[q], g1_send.at[q], g1_recv.at[q], (t, mate)
            )
        )
    over = []
    for q in range(quarters):
        near[q].wait_recv()
        half[q] = (
            canvas[q, core, 1 - row].astype(f32) + c_in[q, 1 - row].astype(f32)
        ).astype(bf16)
        over.append(launch(half.at[q], half_in.at[q], g2_send.at[q], g2_recv.at[q], (t, cross)))
    for q in range(quarters):
        over[q].wait_recv()
        value = (
            canvas[q, core, row].astype(f32) + c_in[q, row].astype(f32) + half_in[q].astype(f32)
        ).astype(bf16)
        for u in range(part // rows):
            for plane in range(2):
                mine[q * (part // rows) + u, plane] = value[
                    plane * part + u * rows : plane * part + (u + 1) * rows
                ]
    for d in range(1, tiles):
        launch(
            mine.at[order[d]], rows_in.at[t], g3_send.at[d], g3_recv.at[t], (order[d], m)
        )
    numer = mine[t].astype(f32)
    for d in range(1, tiles):
        remote(
            mine.at[order[d]], rows_in.at[order[d]], g3_send.at[d], g3_recv.at[order[d]], (order[d], m)
        ).wait_recv()
        numer = numer + rows_in[order[d]].astype(f32)
    scale = 1.0 / (denom + rho_weight)
    for o in range(2):
        value = (numer[o] + rho_weight * (aux_next[o] - dual[o])) * scale
        obj_next[o] = value
        dual_next[o] = dual[o] + value - aux_next[o]
    for copy in sent:
        copy.wait_send()


def fast_device(
    obj_x,
    dual_u,
    probes,
    intensity,
    corners,
    owner,
    w_in,
    b_in,
    w_down,
    b_down,
    w_mid,
    b_mid,
    w_out,
    b_out,
):
    tiles = lax.axis_size("tile")
    modes = lax.axis_size("mode")
    rows, cols = obj_x.shape[1], obj_x.shape[2]
    patch = probes.shape[-1]
    chans = w_in.shape[1]
    phases = jnp.asarray(tap_phases(), jnp.bfloat16)
    big_in = jnp.einsum("tasp,toc->aospc", phases, w_in).reshape(4 * chans, 72)
    big_out = jnp.einsum("tasp,toc->saopc", phases, w_out).reshape(72, 4 * chans)
    big_down = jnp.transpose(w_down, (1, 0, 2)).reshape(chans, 4 * chans)
    big_mid = jnp.transpose(w_mid, (1, 0, 2)).reshape(chans, 9 * chans)
    f32 = jnp.float32
    bf16 = jnp.bfloat16
    vmem = pl.BlockSpec(memory_space=pltpu.VMEM)
    smem = pl.BlockSpec(memory_space=pltpu.SMEM)
    quarters = 4
    part = patch // quarters
    edge = 16
    coarse = rows // 2 + HALO
    dma = pltpu.SemaphoreType.DMA
    block = jax.ShapeDtypeStruct((2, rows, cols), f32)
    return pl.pallas_call(
        functools.partial(fast_kernel, tiles, modes),
        out_shape=(block, block, block, jax.ShapeDtypeStruct((1,), f32)),
        in_specs=[smem] * 3 + [vmem] * 15,
        out_specs=(vmem, vmem, vmem, smem),
        scratch_shapes=[
            pltpu.VMEM((modes, tiles, 2, rows, cols), bf16),
            pltpu.VMEM((3, 2, rows + 2 * edge, cols), bf16),
            pltpu.VMEM((rows, patch), f32),
            pltpu.VMEM((modes - 1, rows, patch), f32),
            pltpu.VMEM((4, rows + 2 * edge, cols), f32),
            pltpu.VMEM((8, coarse * cols), f32),
            pltpu.VMEM((8, rows // 2, cols), f32),
            pltpu.VMEM((2, rows, cols), f32),
            pltpu.VMEM((patch, 2 * patch), f32),
            pltpu.VMEM((quarters, part, patch), bf16),
            pltpu.VMEM((quarters, part, patch), bf16),
            pltpu.VMEM((quarters, part, patch), bf16),
            pltpu.VMEM((quarters, part, patch), bf16),
            pltpu.VMEM((2 * patch, patch), bf16),
            pltpu.VMEM((2 * patch, patch), bf16),
            pltpu.VMEM((quarters, 2, modes // 2, 2 * part, cols), bf16),
            pltpu.VMEM((quarters, modes // 2, 2 * part, cols), bf16),
            pltpu.VMEM((quarters, 2 * part, cols), bf16),
            pltpu.VMEM((quarters, 2 * part, cols), bf16),
            pltpu.VMEM((tiles, 2, rows, cols), bf16),
            pltpu.VMEM((tiles, 2, rows, cols), bf16),
        ]
        + [dma((tiles,))] * 8
        + [dma((8,))] * 2
        + [dma((modes - 1,))] * 2
        + [dma((quarters,))] * 8
        + [dma((tiles,))] * 2,
        compiler_params=pltpu.CompilerParams(
            collective_id=0, has_side_effects=True, vmem_limit_bytes=40 * 1024 * 1024
        ),
    )(
        corners,
        owner,
        b_out,
        obj_x,
        dual_u,
        probes,
        intensity,
        *[jnp.asarray(part_of) for part_of in table_parts(patch)],
        big_in,
        jnp.tile(b_in, 4)[:, None],
        big_down,
        b_down[:, None],
        big_mid,
        b_mid[:, None],
        big_out,
    )


def per_device(obj_x, dual_u, probes, intensity, corners, owner, *weights):
    tiles = lax.axis_size("tile")
    modes = lax.axis_size("mode")
    fits = (
        obj_x.shape[1] * tiles == probes.shape[-1]
        and intensity.shape[0] == 1
        and owner.shape[0] == tiles
        and modes == 4
        and tiles > 2
        and probes.shape[0] == 1
        and obj_x.shape[1] % 32 == 0
        and obj_x.shape[2] % 128 == 0
        and probes.shape[-1] // 4 % obj_x.shape[1] == 0
    )
    run = fast_device if fits else general_device
    return run(obj_x, dual_u, probes, intensity, corners, owner, *weights)


def solution(mesh):
    return jax.shard_map(
        per_device,
        mesh=mesh,
        in_specs=(
            P(None, "tile", "mode"),
            P(None, "tile", "mode"),
            P("mode", None, None, None),
            P("tile", None, None),
            P(),
            P(),
            P(),
            P(),
            P(),
            P(),
            P(),
            P(),
            P(),
            P(),
        ),
        out_specs=(
            P(None, "tile", "mode"),
            P(None, "tile", "mode"),
            P(None, "tile", "mode"),
            P("tile"),
        ),
        check_vma=False,
    )
```
